256 devices in a mesh: dp: 64 (over z, x_hi, y), tensor: 4 (over x_lo, core).
Axes of the slice: x: 4 (x_hi: 2, x_lo: 2; x = x_hi * 2 + x_lo), y: 4, z: 8, core: 2. Of those that a mesh axis runs over, the one named last changes fastest.
Arguments:
- image_embed: bfloat16 [65536, 1152], P('dp'), may hold values from -6 to 6
- text_feature: bfloat16 [65536, 1152], P('dp', 'tensor'), may hold values from -6 to 6
- projection: bfloat16 [1152, 1152], P('tensor'), may hold values from -0.1875 to 0.1875
- logit_scale: float32 [1], replicated, may hold values from 8 to 30
- logit_bias: float32 [1], replicated, may hold values from -3 to -1
- partner_masks: int32 [3], replicated, may hold values from 1 to 32, as said below
Outputs:
- image_grad: float32 [65536, 1152], P(('dp', 'tensor'))
- text_grad: float32 [65536, 1152], P(('dp', 'tensor'))
- feature_grad: float32 [65536, 1152], P('dp', 'tensor')
The draws below stay inside these ranges and needn't reach their ends.
Inputs may be any that keep to these rules, and one draw needn't show every extreme that they name: `partner_masks`: the entries are distinct powers of two, and 32 is among them.
All inputs are finite; a program needn't handle non-finite values.
Results may differ from the reference program's by a relative error of at most 0.022.
Values may be sent and summed in bfloat16 or wider, within the bound.
A program may use at most 128 MiB of HBM per device.

```python
import math
import jax
import jax.numpy as jnp
from jax import lax

D = 1152
E = 1152
ROWS = 1024
ROUNDS = 3
TOKENS = 65536
N_DP = 64
N_TENSOR = 4


def draw_partner_masks(key, part):
    key = jax.random.fold_in(key, 7)
    bit_count = N_DP.bit_length() - 1
    first_key, second_key = jax.random.split(key)
    lower = jax.random.permutation(first_key, bit_count - 1)[:ROUNDS - 1]
    chosen = jnp.concatenate([lower.astype(jnp.int32), jnp.array([bit_count - 1], jnp.int32)])
    chosen = jax.random.permutation(second_key, chosen)
    return jnp.left_shift(jnp.int32(1), chosen.astype(jnp.int32)).astype(jnp.int32)


def block_scale(stream_key, shape, pieces, smallest, top_value):
    loudness, own = 1.0, jax.random.fold_in(stream_key, 6)
    for dim, blocks in pieces:
        steps = jnp.exp(jax.random.uniform(jax.random.fold_in(own, dim), (blocks,), jnp.float32, smallest / len(pieces), top_value / len(pieces)))
        loudness = loudness * jnp.repeat(steps, shape[dim] // blocks).reshape([-1 if axis == dim else 1 for axis in range(len(shape))])
    return loudness


def normal_values(stream_key, extent, scale, reach, cuts=(), kind=jnp.bfloat16):
    loudness = block_scale(stream_key, extent, cuts, -0.22, 0.18) if cuts else 1.0
    drawn = jax.random.normal(stream_key, extent, jnp.float32) * scale * loudness
    return jnp.minimum(jnp.maximum(drawn, -reach), reach).astype(kind)


def setup_inputs(seed: int = 0) -> dict:
    arg_keys = jax.random.split(jax.random.key(seed), 7)
    return {
        "image_embed": normal_values(arg_keys[0], (TOKENS, E), 1.0, 6.0, ((0, 64),)),
        "text_feature": normal_values(arg_keys[1], (TOKENS, D), 1.0, 6.0, ((0, 64), (1, 4))),
        "projection": normal_values(arg_keys[2], (D, E), D ** -0.5, 0.1875, ((0, 4),)),
        "logit_scale": jnp.clip(jnp.exp(jax.random.uniform(arg_keys[3], (1,), jnp.float32, math.log(8.0), math.log(30.0))), 8.0, 30.0),
        "logit_bias": jnp.clip(jax.random.uniform(arg_keys[4], (1,), jnp.float32, -3.0, -1.0), -3.0, -1.0),
        "partner_masks": draw_partner_masks(jax.random.fold_in(arg_keys[6], 71), 0),
    }


EPSILON = 1e-06

def unit_rows(values):
    wide = values.astype(jnp.float32)
    length = jnp.sqrt(lax.optimization_barrier(jnp.sum(wide * wide, axis=1, keepdims=True)) + EPSILON)
    return (wide / length, length)

def pair_coeffs(dots, signs, scale_value, bias_value):
    logits = scale_value * dots + bias_value
    return (-signs * scale_value * jax.nn.sigmoid(-signs * logits)).astype(jnp.bfloat16)

def low_sum(values):
    return lax.optimization_barrier(values.astype(jnp.bfloat16)).astype(jnp.float32)

def reference(image_embed, text_feature, projection, logit_scale, logit_bias, partner_masks):
    share = ROWS // N_TENSOR
    width_part = D // N_TENSOR
    text_raw = jnp.zeros((ROWS * N_DP, E), jnp.float32)
    for block in range(N_TENSOR):
        piece = jnp.dot(text_feature[:, block * width_part:(block + 1) * width_part], projection[block * width_part:(block + 1) * width_part], preferred_element_type=jnp.float32)
        text_raw = text_raw + low_sum(piece)
    text_unit, text_norm = unit_rows(text_raw)
    image_unit, image_norm = unit_rows(image_embed)
    text_low = text_unit.astype(jnp.bfloat16).reshape(N_DP, ROWS, E)
    image_low = image_unit.astype(jnp.bfloat16).reshape(N_DP, ROWS, E)
    scale_value = logit_scale[0]
    bias_value = logit_bias[0]
    positions = jnp.arange(ROWS, dtype=jnp.int32)
    signs_own = jnp.where(positions[:, None] == positions[None, :], 1.0, -1.0).astype(jnp.float32)
    contract_rows = (((0,), (0,)), ((), ()))

    def by_blocks(coeffs, texts):
        return jnp.einsum('ikj,kje->kie', coeffs.astype(jnp.float32).reshape(ROWS, N_TENSOR, share), texts.astype(jnp.float32).reshape(N_TENSOR, share, E))

    def one_group(group):
        images = image_low[group]
        texts = text_low[group]
        coeffs = pair_coeffs(jnp.dot(images, texts.T, preferred_element_type=jnp.float32), signs_own, scale_value, bias_value)
        image_parts = by_blocks(coeffs, texts)
        text_dir = lax.dot_general(coeffs, images, contract_rows, preferred_element_type=jnp.float32)
        for turn in range(ROUNDS):
            partner = jnp.bitwise_xor(group, partner_masks[turn])
            other_texts = text_low[partner]
            other_images = image_low[partner]
            forward = pair_coeffs(jnp.dot(images, other_texts.T, preferred_element_type=jnp.float32), -1.0, scale_value, bias_value)
            image_parts = image_parts + by_blocks(forward, other_texts)
            mirror = pair_coeffs(jnp.dot(other_images, texts.T, preferred_element_type=jnp.float32), -1.0, scale_value, bias_value)
            text_dir = text_dir + low_sum(lax.dot_general(mirror, other_images, contract_rows, preferred_element_type=jnp.float32))
        image_dir = lax.optimization_barrier(jnp.sum(low_sum(image_parts), axis=0))
        return (image_dir, text_dir)
    image_dir, text_dir = lax.map(one_group, jnp.arange(N_DP, dtype=jnp.int32))
    image_dir = image_dir.reshape(N_DP * ROWS, E)
    text_dir = text_dir.reshape(N_DP * ROWS, E)
    image_grad = (image_dir - image_unit * lax.optimization_barrier(jnp.sum(image_unit * image_dir, axis=1, keepdims=True))) / image_norm
    text_grad = (text_dir - text_unit * lax.optimization_barrier(jnp.sum(text_unit * text_dir, axis=1, keepdims=True))) / text_norm
    feature_grad = jnp.dot(text_grad.astype(jnp.bfloat16), projection.T, preferred_element_type=jnp.float32)
    return (image_grad, text_grad, feature_grad)
```

```python
import functools
import itertools

import jax
import jax.numpy as jnp
from jax import lax
from jax.experimental import pallas as pl
from jax.experimental.pallas import tpu as pltpu
from jax.sharding import PartitionSpec as P

EPSILON = 1e-06
MESH = pl.DeviceIdType.MESH
FAR = 32
NEAR = (1, 2, 4, 8, 16)
PAIRS = tuple(itertools.combinations(NEAR, 2))
F32 = jnp.float32
BF16 = jnp.bfloat16
LAST = (((1,), (1,)), ((), ()))
FIRST = (((0,), (0,)), ((), ()))


def flipped(index, bit):
    return index + bit - 2 * bit * (index // bit % 2)


def inverse_norm(values):
    return 1.0 / jnp.sqrt(jnp.sum(values * values, axis=1, keepdims=True) + EPSILON)


def kernel(
    near,
    scale_ref,
    bias_ref,
    image_ref,
    feature_ref,
    projection_ref,
    image_grad_ref,
    text_grad_ref,
    feature_grad_ref,
    image_low,
    proj,
    feature_in,
    feature_rows,
    text_raw,
    text_low,
    image_dir,
    text_dir,
    grad_acc,
    grad_out,
    grad_in,
    reduce_out,
    reduce_in,
    block_out,
    block_in,
    send_sem,
    recv_sem,
):
    rows, width = image_ref.shape
    part = feature_ref.shape[1]
    share = rows // 4
    half = share // 2
    dp = lax.axis_index("dp")
    slot = lax.axis_index("tensor")
    core = slot % 2
    side = slot // 2
    tensor_peer = [
        slot,
        2 * side + 1 - core,
        2 * (1 - side) + core,
        2 * (1 - side) + 1 - core,
    ]
    partners = (FAR,) + near
    place = [(flipped(dp, mask), slot) for mask in partners]
    across = (flipped(dp, 4), tensor_peer[2])
    mates = [(dp, tensor_peer[i]) for i in range(4)]

    used = [0]

    def copy(source, target, device):
        number = used[0]
        used[0] += 1
        return pltpu.make_async_remote_copy(
            src_ref=source,
            dst_ref=target,
            send_sem=send_sem.at[number],
            recv_sem=recv_sem.at[number],
            device_id=device,
            device_id_type=MESH,
        )

    scale = scale_ref[0]
    bias = bias_ref[0]

    barrier = pltpu.get_barrier_semaphore()
    everyone = mates[1:] + [across] + place
    for device in everyone:
        pl.semaphore_signal(barrier, inc=1, device_id=device, device_id_type=MESH)

    proj[pl.ds(0, part), :] = projection_ref[...]
    pl.semaphore_wait(barrier, len(everyone))

    features = [[None] * 4 for _ in range(2)]
    for piece in range(2):
        for i in (2, 3, 1):
            start = pl.multiple_of(tensor_peer[i] * share + piece * half, half)
            features[piece][i] = copy(
                feature_ref.at[pl.ds(start, half), :],
                feature_in.at[i - 1, pl.ds(piece * half, half), :],
                mates[i],
            )
            features[piece][i].start()
    cut = part // 2
    proj_core = copy(projection_ref, proj.at[pl.ds(part, part), :], mates[1])
    proj_near = copy(
        projection_ref.at[pl.ds(0, cut), :], proj.at[pl.ds(2 * part, cut), :], mates[2]
    )
    proj_wrap = copy(
        projection_ref.at[pl.ds(cut, cut), :],
        proj.at[pl.ds(2 * part + cut, cut), :],
        across,
    )
    for c in (proj_near, proj_wrap, proj_core):
        c.start()

    def normalize(tile, _):
        at = pl.ds(pl.multiple_of(tile * 128, 128), 128)
        wide = image_ref[at, :].astype(F32)
        image_low[at, :] = (wide * inverse_norm(wide)).astype(BF16)
        return 0

    lax.fori_loop(0, rows // 128, normalize, 0)

    texts = [[None] * 3 for _ in range(2)]
    for piece in range(2):
        at = pl.ds(piece * half, half)
        for i in (2, 3, 1):
            features[piece][i].wait_recv()
        mine = pl.ds(pl.multiple_of(slot * share + piece * half, half), half)
        feature_rows[0, at, :] = jnp.concatenate(
            [feature_ref[mine, :]] + [feature_in[i, at, :] for i in range(3)], axis=1
        )
        for r in range(3):
            texts[piece][r] = copy(
                feature_rows.at[0, at, :], feature_rows.at[r + 1, at, :], place[r]
            )
            texts[piece][r].start()

    proj_near.wait_recv()
    pass_near = copy(
        proj.at[pl.ds(2 * part, cut), :], proj.at[pl.ds(3 * part, cut), :], mates[1]
    )
    pass_near.start()
    proj_wrap.wait_recv()
    pass_wrap = copy(
        proj.at[pl.ds(2 * part + cut, cut), :],
        proj.at[pl.ds(3 * part + cut, cut), :],
        mates[1],
    )
    pass_wrap.start()
    proj_core.wait_recv()
    pass_near.wait_recv()
    pass_wrap.wait_recv()

    def project(source, at, keep):
        raw = jnp.dot(feature_rows[source, at, :], proj[...], preferred_element_type=F32)
        if keep:
            text_raw[at, :] = raw
        text_low[at, :] = (raw * inverse_norm(raw)).astype(BF16)

    def window(at, count, grads, own):
        grads[at, :] = jnp.zeros((count, width), F32)

        def step(tile, _):
            images = pl.ds(pl.multiple_of(tile * share, share), share)
            image = image_low[images, :]
            text = text_low[at, :]
            logits = scale * lax.dot_general(image, text, LAST, preferred_element_type=F32) + bias
            if own:
                line = lax.broadcasted_iota(jnp.int32, logits.shape, 0)
                column = lax.broadcasted_iota(jnp.int32, logits.shape, 1)
                same = line + (tile - slot) * share == column
                value = scale / (1.0 + jnp.exp(jnp.where(same, logits, -logits)))
                coeffs = jnp.where(same, -value, value).astype(BF16)
            else:
                coeffs = (scale / (1.0 + jnp.exp(-logits))).astype(BF16)
            direction = jnp.dot(coeffs, text, preferred_element_type=F32)
            if own:
                image_dir[images, :] = direction
            else:
                image_dir[images, :] += direction
            grads[at, :] += lax.dot_general(coeffs, image, FIRST, preferred_element_type=F32)
            return 0

        lax.fori_loop(0, rows // share, step, 0)

    whole = pl.ds(0, share)
    project(0, whole, True)
    window(whole, share, text_dir, True)

    returns = [[None] * 3 for _ in range(2)]
    for r in (1, 2):
        for piece in range(2):
            texts[piece][r].wait_recv()
        project(r + 1, whole, False)
        window(whole, share, grad_acc, False)
        grad_out[r] = grad_acc[...].astype(BF16)
        for piece in range(2):
            at = pl.ds(piece * half, half)
            returns[piece][r] = copy(grad_out.at[r, at, :], grad_in.at[r, at, :], place[r])
            returns[piece][r].start()
    for piece in range(2):
        at = pl.ds(piece * half, half)
        texts[piece][0].wait_recv()
        project(1, at, False)
        window(at, half, grad_acc, False)
        grad_out[0, at, :] = grad_acc[at, :].astype(BF16)
        returns[piece][0] = copy(grad_out.at[0, at, :], grad_in.at[0, at, :], place[0])
        returns[piece][0].start()

    def block(index):
        return pl.ds(pl.multiple_of(index * share, share), share)

    reduce_out[0] = image_dir[block(tensor_peer[3]), :].astype(BF16)
    reduce_far = copy(reduce_out.at[0], reduce_in.at[0], mates[1])
    reduce_far.start()
    reduce_out[1] = image_dir[block(tensor_peer[1]), :].astype(BF16)
    reduce_core = copy(reduce_out.at[1], reduce_in.at[1], mates[1])
    reduce_core.start()
    reduce_far.wait_recv()
    reduce_out[2] = (image_dir[block(tensor_peer[2]), :] + reduce_in[0].astype(F32)).astype(BF16)
    reduce_cross = copy(reduce_out.at[2], reduce_in.at[2], mates[2])
    reduce_cross.start()

    blocks = [[None] * 4 for _ in range(2)]

    def finish_text(piece):
        at = pl.ds(piece * half, half)
        for r in (1, 2, 0):
            returns[piece][r].wait_recv()
        raw = text_raw[at, :]
        scaled = inverse_norm(raw)
        unit = raw * scaled
        total = text_dir[at, :] + grad_in[0, at, :].astype(F32)
        total = total + grad_in[1, at, :].astype(F32) + grad_in[2, at, :].astype(F32)
        grad = (total - unit * jnp.sum(unit * total, axis=1, keepdims=True)) * scaled
        text_grad_ref[at, :] = grad
        low = grad.astype(BF16)
        for i in (2, 3, 1, 0):
            value = lax.dot_general(
                low, proj[pl.ds(i * part, part), :], LAST, preferred_element_type=F32
            )
            if i == 0:
                mine = pl.ds(pl.multiple_of(slot * share + piece * half, half), half)
                feature_grad_ref[mine, :] = value
            else:
                block_out[i - 1, at, :] = value.astype(BF16)
                blocks[piece][i] = copy(
                    block_out.at[i - 1, at, :], block_in.at[i - 1, at, :], mates[i]
                )
                blocks[piece][i].start()

    finish_text(0)

    reduce_core.wait_recv()
    reduce_cross.wait_recv()
    own = block(slot)
    wide = image_ref[own, :].astype(F32)
    scaled = inverse_norm(wide)
    unit = wide * scaled
    total = image_dir[own, :] + reduce_in[1].astype(F32) + reduce_in[2].astype(F32)
    image_grad_ref[...] = (total - unit * jnp.sum(unit * total, axis=1, keepdims=True)) * scaled

    finish_text(1)

    for piece in range(2):
        for i in (1, 2, 3):
            blocks[piece][i].wait_recv()
            there = pl.ds(pl.multiple_of(tensor_peer[i] * share + piece * half, half), half)
            feature_grad_ref[there, :] = block_in[i - 1, pl.ds(piece * half, half), :].astype(F32)

    for piece in range(2):
        for i in (1, 2, 3):
            features[piece][i].wait_send()
            blocks[piece][i].wait_send()
        for r in range(3):
            texts[piece][r].wait_send()
            returns[piece][r].wait_send()
    for c in (proj_core, proj_near, proj_wrap, pass_near, pass_wrap):
        c.wait_send()
    for c in (reduce_far, reduce_core, reduce_cross):
        c.wait_send()


COPIES = 32


def fused(number, near, scale, bias, image, feature, projection):
    rows, width = image.shape
    part = feature.shape[1]
    share = rows // 4
    vmem = pl.BlockSpec(memory_space=pltpu.VMEM)
    smem = pl.BlockSpec(memory_space=pltpu.SMEM)
    return pl.pallas_call(
        functools.partial(kernel, near),
        out_shape=(
            jax.ShapeDtypeStruct((share, width), F32),
            jax.ShapeDtypeStruct((share, width), F32),
            jax.ShapeDtypeStruct((rows, part), F32),
        ),
        in_specs=[smem, smem, vmem, vmem, vmem],
        out_specs=[vmem, vmem, vmem],
        scratch_shapes=[
            pltpu.VMEM((rows, width), BF16),
            pltpu.VMEM((4 * part, width), BF16),
            pltpu.VMEM((3, share, part), BF16),
            pltpu.VMEM((4, share, width), BF16),
            pltpu.VMEM((share, width), F32),
            pltpu.VMEM((share, width), BF16),
            pltpu.VMEM((rows, width), F32),
            pltpu.VMEM((share, width), F32),
            pltpu.VMEM((share, width), F32),
            pltpu.VMEM((3, share, width), BF16),
            pltpu.VMEM((3, share, width), BF16),
            pltpu.VMEM((3, share, width), BF16),
            pltpu.VMEM((3, share, width), BF16),
            pltpu.VMEM((3, share, part), BF16),
            pltpu.VMEM((3, share, part), BF16),
            pltpu.SemaphoreType.DMA((COPIES,)),
            pltpu.SemaphoreType.DMA((COPIES,)),
        ],
        compiler_params=pltpu.CompilerParams(
            collective_id=number, has_side_effects=True, vmem_limit_bytes=56 * 1024 * 1024
        ),
    )(scale, bias, image, feature, projection)


def per_device(image_embed, text_feature, projection, logit_scale, logit_bias, partner_masks):
    sums = jnp.array([sum(pair) for pair in PAIRS], jnp.int32)
    chosen = jnp.sum(partner_masks) - FAR
    which = jnp.sum(jnp.where(sums == chosen, jnp.arange(len(PAIRS), dtype=jnp.int32), 0))
    return lax.switch(
        which,
        [functools.partial(fused, number, pair) for number, pair in enumerate(PAIRS)],
        logit_scale,
        logit_bias,
        image_embed,
        text_feature,
        projection,
    )


def solution(mesh):
    return jax.shard_map(
        per_device,
        mesh=mesh,
        in_specs=(P("dp", None), P("dp", "tensor"), P("tensor", None), P(), P(), P()),
        out_specs=(P(("dp", "tensor"), None), P(("dp", "tensor"), None), P("dp", "tensor")),
        check_vma=False,
    )
```

```python
import functools
import itertools

import jax
import jax.numpy as jnp
from jax import lax
from jax.experimental import pallas as pl
from jax.experimental.pallas import tpu as pltpu
from jax.sharding import PartitionSpec as P

EPSILON = 1e-06
MESH = pl.DeviceIdType.MESH
FAR = 32
STRIP = 64
NEAR = (1, 2, 4, 8, 16)
PAIRS = tuple(itertools.combinations(NEAR, 2))
F32 = jnp.float32
BF16 = jnp.bfloat16
LAST = (((1,), (1,)), ((), ()))
FIRST = (((0,), (0,)), ((), ()))


def flipped(index, bit):
    return index + bit - 2 * bit * (index // bit % 2)


def order_of(near):
    along = [mask for mask in near if mask >= 8]
    rest = [mask for mask in near if mask < 8]
    if not along:
        return (near[0], FAR, near[1])
    return tuple(rest + along + [FAR])


def inverse_norm(values):
    return 1.0 / jnp.sqrt(jnp.sum(values * values, axis=1, keepdims=True) + EPSILON)


def kernel(
    near,
    scale_ref,
    bias_ref,
    image_hbm,
    feature_hbm,
    projection_hbm,
    image_grad_ref,
    text_grad_ref,
    feature_grad_ref,
    image_ref,
    image_low,
    proj,
    feature_rows,
    text_raw,
    text_low,
    image_dir,
    text_dir,
    grad_out,
    grad_in,
    reduce_out,
    reduce_in,
    block_out,
    block_in,
    send_sem,
    recv_sem,
    text_send,
    text_recv,
    grad_send,
    grad_recv,
    block_send,
    block_recv,
    local_sem,
):
    rows, width = image_ref.shape
    part = feature_hbm.shape[0]
    share = rows // 4
    half = share // 2
    dp = lax.axis_index("dp")
    slot = lax.axis_index("tensor")
    core = slot % 2
    side = slot // 2
    peer = [
        slot,
        2 * side + 1 - core,
        2 * (1 - side) + core,
        2 * (1 - side) + 1 - core,
    ]
    turns = order_of(near)
    place = [flipped(dp, mask) for mask in turns]
    urgent = sorted(range(3), key=lambda r: (turns[r] < 8, r))
    across = (flipped(dp, 4), peer[2])
    mates = [(dp, peer[i]) for i in range(4)]

    def between(source, target, device, sent, received):
        return pltpu.make_async_remote_copy(
            src_ref=source,
            dst_ref=target,
            send_sem=sent,
            recv_sem=received,
            device_id=device,
            device_id_type=MESH,
        )

    used = [0]

    def copy(source, target, device):
        number = used[0]
        used[0] += 1
        return between(source, target, device, send_sem.at[number], recv_sem.at[number])

    def local(source, target, number):
        return pltpu.make_async_copy(source, target, local_sem.at[number])

    def block(index):
        return pl.ds(pl.multiple_of(index * share, share), share)

    def piece_of(index, piece):
        return pl.ds(pl.multiple_of(index * share + piece * half, half), half)

    def strip(tile):
        return pl.ds(pl.multiple_of(tile * STRIP, STRIP), STRIP)

    def outgoing_image(number, owner, add):
        def shorten(tile, _):
            here = pl.ds(pl.multiple_of(owner * share + tile * STRIP, STRIP), STRIP)
            value = image_dir[here, :]
            if add:
                value = value + reduce_in[0, strip(tile), :].astype(F32)
            reduce_out[number, strip(tile), :] = value.astype(BF16)
            return 0

        lax.fori_loop(0, share // STRIP, shorten, 0)

    scale = scale_ref[0]
    bias = bias_ref[0]

    barrier = pltpu.get_barrier_semaphore()
    everyone = mates[1:] + [across] + [(index, slot) for index in place]
    for device in everyone:
        pl.semaphore_signal(barrier, inc=1, device_id=device, device_id_type=MESH)

    own_proj = local(projection_hbm, proj.at[pl.ds(0, part), :], 0)
    own_feature = local(
        feature_hbm.at[:, block(slot)], feature_rows.at[0, pl.ds(0, part), :], 1
    )
    own_image = local(image_hbm, image_ref, 2)
    for c in (own_feature, own_proj, own_image):
        c.start()
    pl.semaphore_wait(barrier, len(everyone))

    def text_copy(r, i):
        device = place[0] + r * (2 - r) * (place[1] - place[0])
        device = device + r * (r - 1) // 2 * (place[2] - place[0])
        rows_at = pl.ds(i * part, part)
        return between(
            feature_hbm.at[:, block(slot)] if i == 0 else feature_rows.at[0, rows_at, :],
            feature_rows.at[r + 1, rows_at, :],
            (device, slot),
            text_send.at[r * 4 + i],
            text_recv.at[r * 4 + i],
        )

    features = [None] * 4
    for i in (2, 3, 1):
        features[i] = copy(
            feature_hbm.at[:, block(peer[i])],
            feature_rows.at[0, pl.ds(i * part, part), :],
            mates[i],
        )
        features[i].start()
    for r in urgent:
        text_copy(r, 0).start()
    cut = part // 18 * 5
    rest = part - cut
    proj_wrap = copy(
        projection_hbm.at[pl.ds(cut, rest), :], proj.at[pl.ds(2 * part + cut, rest), :], across
    )
    proj_core = copy(projection_hbm, proj.at[pl.ds(part, part), :], mates[1])
    proj_near = copy(
        projection_hbm.at[pl.ds(0, cut), :], proj.at[pl.ds(2 * part, cut), :], mates[2]
    )
    proj_wrap.start()
    proj_core.start()

    def grad_copy(r, piece):
        at = pl.ds(pl.multiple_of(piece * half, half), half)
        device = place[0] + r * (2 - r) * (place[1] - place[0])
        device = device + r * (r - 1) // 2 * (place[2] - place[0])
        return between(
            grad_out.at[r, at, :],
            grad_in.at[r, at, :],
            (device, slot),
            grad_send.at[r * 2 + piece],
            grad_recv.at[r * 2 + piece],
        )

    def block_copy(i, piece):
        at = pl.ds(pl.multiple_of(piece * half, half), half)
        return between(
            block_out.at[i - 1, :, at],
            block_in.at[i - 1, :, at],
            mates[i],
            block_send.at[(i - 1) * 2 + piece],
            block_recv.at[(i - 1) * 2 + piece],
        )

    for i in (1, 2, 3):
        features[i].wait_recv()
        for r in urgent:
            text_copy(r, i).start()
    proj_near.start()
    own_feature.wait()

    own_image.wait()

    def normalize(tile, _):
        at = strip(tile)
        wide = image_ref[at, :].astype(F32)
        image_low[at, :] = (wide * inverse_norm(wide)).astype(BF16)
        image_dir[at, :] = jnp.zeros((STRIP, width), F32)
        return 0

    lax.fori_loop(0, rows // STRIP, normalize, 0)

    proj_wrap.wait_recv()
    pass_wrap = copy(
        proj.at[pl.ds(2 * part + cut, rest), :],
        proj.at[pl.ds(3 * part + cut, rest), :],
        mates[1],
    )
    pass_wrap.start()
    proj_near.wait_recv()
    pass_near = copy(
        proj.at[pl.ds(2 * part, cut), :], proj.at[pl.ds(3 * part, cut), :], mates[1]
    )
    pass_near.start()
    own_proj.wait()
    proj_core.wait_recv()
    pass_wrap.wait_recv()
    pass_near.wait_recv()

    def window(unit, _):
        other = (unit + 3) // 4

        @pl.when(unit > 0)
        def _():
            for i in range(4):
                text_copy(unit - 1, i).wait_recv()

        raw = lax.dot_general(
            feature_rows[unit], proj[...], FIRST, preferred_element_type=F32
        )
        text_raw[other] = raw

        def unit_text(tile, _):
            at = strip(tile)
            wide = text_raw[other, at, :]
            text_low[at, :] = (wide * inverse_norm(wide)).astype(BF16)
            text_dir[other, at, :] = jnp.zeros((STRIP, width), F32)
            return 0

        lax.fori_loop(0, share // STRIP, unit_text, 0)

        def step(tile, _):
            images = block(tile)
            image = image_low[images, :]
            text = text_low[...]
            logits = scale * lax.dot_general(image, text, LAST, preferred_element_type=F32) + bias
            line = lax.broadcasted_iota(jnp.int32, logits.shape, 0)
            column = lax.broadcasted_iota(jnp.int32, logits.shape, 1)
            same = line - column == (slot - tile) * share - unit * 4 * rows
            value = scale / (1.0 + jnp.exp(jnp.where(same, logits, -logits)))
            coeffs = jnp.where(same, -value, value).astype(BF16)
            image_dir[images, :] += jnp.dot(coeffs, text, preferred_element_type=F32)
            text_dir[other] += lax.dot_general(coeffs, image, FIRST, preferred_element_type=F32)
            return 0

        lax.fori_loop(0, rows // share, step, 0)

        @pl.when(unit > 0)
        def _():
            def shorten(tile, _):
                grad_out[unit - 1, strip(tile), :] = text_dir[1, strip(tile), :].astype(BF16)
                return 0

            lax.fori_loop(0, share // STRIP, shorten, 0)
            grad_copy(unit - 1, 0).start()
            grad_copy(unit - 1, 1).start()

        return 0

    lax.fori_loop(0, 4, window, 0)

    outgoing_image(0, peer[3], False)
    reduce_far = copy(reduce_out.at[0], reduce_in.at[0], mates[1])
    reduce_far.start()
    outgoing_image(1, peer[1], False)
    reduce_core = copy(reduce_out.at[1], reduce_in.at[1], mates[1])
    reduce_core.start()
    reduce_far.wait_recv()
    outgoing_image(2, peer[2], True)
    reduce_cross = copy(reduce_out.at[2], reduce_in.at[2], mates[2])
    reduce_cross.start()
    reduce_core.wait_recv()
    reduce_cross.wait_recv()

    def finish_image(tile, _):
        at = strip(tile)
        here = pl.ds(pl.multiple_of(slot * share + tile * STRIP, STRIP), STRIP)
        wide = image_ref[here, :].astype(F32)
        scaled = inverse_norm(wide)
        unit = wide * scaled
        total = image_dir[here, :] + reduce_in[1, at, :].astype(F32)
        total = total + reduce_in[2, at, :].astype(F32)
        total = total - unit * jnp.sum(unit * total, axis=1, keepdims=True)
        image_grad_ref[at, :] = total * scaled
        return 0

    lax.fori_loop(0, share // STRIP, finish_image, 0)

    def finish_text(piece, _):
        at = pl.ds(pl.multiple_of(piece * half, half), half)
        for r in (0, 2, 1):
            grad_copy(r, piece).wait_recv()

        def rows_done(tile, _):
            here = pl.ds(pl.multiple_of(piece * half + tile * STRIP, STRIP), STRIP)
            raw = text_raw[0, here, :]
            scaled = inverse_norm(raw)
            unit = raw * scaled
            total = text_dir[0, here, :] + grad_in[0, here, :].astype(F32)
            total = total + grad_in[1, here, :].astype(F32) + grad_in[2, here, :].astype(F32)
            total = total - unit * jnp.sum(unit * total, axis=1, keepdims=True)
            text_grad_ref[here, :] = total * scaled
            return 0

        lax.fori_loop(0, half // STRIP, rows_done, 0)
        values = lax.dot_general(
            proj[...], text_grad_ref[at, :].astype(BF16), LAST, preferred_element_type=F32
        )
        for i in (2, 3, 1):
            block_out[i - 1, :, at] = values[i * part : (i + 1) * part].astype(BF16)
            block_copy(i, piece).start()
        feature_grad_ref[:, piece_of(slot, piece)] = values[:part]
        return 0

    lax.fori_loop(0, 2, finish_text, 0)

    for piece in range(2):
        for i in (1, 2, 3):
            block_copy(i, piece).wait_recv()
            feature_grad_ref[:, piece_of(peer[i], piece)] = block_in[
                i - 1, :, pl.ds(piece * half, half)
            ].astype(F32)

    for i in (1, 2, 3):
        features[i].wait_send()
        for piece in range(2):
            block_copy(i, piece).wait_send()
    for r in range(3):
        for i in range(4):
            text_copy(r, i).wait_send()
        for piece in range(2):
            grad_copy(r, piece).wait_send()
    for c in (proj_core, proj_near, proj_wrap, pass_near, pass_wrap):
        c.wait_send()
    for c in (reduce_far, reduce_core, reduce_cross):
        c.wait_send()


def fused(number, near, scale, bias, image, feature, projection):
    rows, width = image.shape
    part = feature.shape[0]
    share = rows // 4
    vmem = pl.BlockSpec(memory_space=pltpu.VMEM)
    smem = pl.BlockSpec(memory_space=pltpu.SMEM)
    any_space = pl.BlockSpec(memory_space=pl.ANY)
    semaphores = [11, 11, 12, 12, 6, 6, 6, 6, 3]
    return pl.pallas_call(
        functools.partial(kernel, near),
        out_shape=(
            jax.ShapeDtypeStruct((share, width), F32),
            jax.ShapeDtypeStruct((share, width), F32),
            jax.ShapeDtypeStruct((part, rows), F32),
        ),
        in_specs=[smem, smem, any_space, any_space, any_space],
        out_specs=[vmem, vmem, vmem],
        scratch_shapes=[
            pltpu.VMEM((rows, width), BF16),
            pltpu.VMEM((rows, width), BF16),
            pltpu.VMEM((4 * part, width), BF16),
            pltpu.VMEM((4, 4 * part, share), BF16),
            pltpu.VMEM((2, share, width), F32),
            pltpu.VMEM((share, width), BF16),
            pltpu.VMEM((rows, width), F32),
            pltpu.VMEM((2, share, width), F32),
            pltpu.VMEM((3, share, width), BF16),
            pltpu.VMEM((3, share, width), BF16),
            pltpu.VMEM((3, share, width), BF16),
            pltpu.VMEM((3, share, width), BF16),
            pltpu.VMEM((3, part, share), BF16),
            pltpu.VMEM((3, part, share), BF16),
        ]
        + [pltpu.SemaphoreType.DMA((count,)) for count in semaphores],
        compiler_params=pltpu.CompilerParams(
            collective_id=number, has_side_effects=True, vmem_limit_bytes=56 * 1024 * 1024
        ),
    )(scale, bias, image, feature, projection)


def per_device(image_embed, text_feature, projection, logit_scale, logit_bias, partner_masks):
    chosen = partner_masks[0] + partner_masks[1] + partner_masks[2] - FAR
    which = jnp.int32(0)
    for number, pair in enumerate(PAIRS):
        which = jnp.where(chosen == sum(pair), number, which)
    image_grad, text_grad, feature_grad = lax.switch(
        which,
        [functools.partial(fused, number, pair) for number, pair in enumerate(PAIRS)],
        logit_scale,
        logit_bias,
        image_embed,
        text_feature.T,
        projection,
    )
    return (image_grad, text_grad, feature_grad.T)


def solution(mesh):
    return jax.shard_map(
        per_device,
        mesh=mesh,
        in_specs=(P("dp", None), P("dp", "tensor"), P("tensor", None), P(), P(), P()),
        out_specs=(P(("dp", "tensor"), None), P(("dp", "tensor"), None), P("dp", "tensor")),
        check_vma=False,
    )
```

```python
import functools
import itertools

import jax
import jax.numpy as jnp
from jax import lax
from jax.experimental import pallas as pl
from jax.experimental.pallas import tpu as pltpu
from jax.sharding import PartitionSpec as P

EPSILON = 1e-06
MESH = pl.DeviceIdType.MESH
FAR = 32
STRIP = 64
NEAR = (1, 2, 4, 8, 16)
PAIRS = tuple(itertools.combinations(NEAR, 2))
F32 = jnp.float32
BF16 = jnp.bfloat16
LAST = (((1,), (1,)), ((), ()))
FIRST = (((0,), (0,)), ((), ()))


def flipped(index, bit):
    return index + bit - 2 * bit * (index // bit % 2)


def stop_of(near):
    return 16 if 16 in near else 8 if 8 in near else 0


def order_of(near):
    stop = stop_of(near)
    if stop:
        return tuple(mask for mask in near if mask != stop) + (FAR, stop)
    if 4 in near:
        return (FAR, 4) + tuple(mask for mask in near if mask != 4)
    return (near[0], FAR, near[1])


def inverse_norm(values):
    return 1.0 / jnp.sqrt(jnp.sum(values * values, axis=1, keepdims=True) + EPSILON)


def kernel(
    near,
    scale_ref,
    bias_ref,
    image_hbm,
    feature_hbm,
    projection_hbm,
    image_grad_ref,
    text_grad_ref,
    feature_grad_ref,
    image_ref,
    image_low,
    proj,
    feature_rows,
    text_raw,
    text_low,
    image_dir,
    text_dir,
    grad_out,
    grad_in,
    reduce_out,
    reduce_in,
    block_out,
    block_in,
    passing,
    relay_in,
    relay_out,
    send_sem,
    recv_sem,
    text_send,
    text_recv,
    grad_send,
    grad_recv,
    block_send,
    block_recv,
    local_sem,
):
    rows, width = image_ref.shape
    part = feature_hbm.shape[0]
    share = rows // 4
    half = share // 2
    dp = lax.axis_index("dp")
    slot = lax.axis_index("tensor")
    core = slot % 2
    side = slot // 2
    peer = [
        slot,
        2 * side + 1 - core,
        2 * (1 - side) + core,
        2 * (1 - side) + 1 - core,
    ]
    turns = order_of(near)
    place = [flipped(dp, mask) for mask in turns]
    stop = stop_of(near)
    urgent = [0] if stop else [r for r in range(3) if turns[r] != 4]
    if stop and turns[0] == 4:
        urgent = []
    late = [r for r in range(3) if turns[r] == 4]
    bit = dp // max(stop, 1) % 2
    near_dp = place[2]
    side_dp = lax.rem(dp + 64 + stop * (2 * bit - 1), 64)
    near_far, side_far = flipped(near_dp, FAR), flipped(side_dp, FAR)
    across = (flipped(dp, 4), peer[2])
    mates = [(dp, peer[i]) for i in range(4)]

    def between(source, target, device, sent, received):
        return pltpu.make_async_remote_copy(
            src_ref=source,
            dst_ref=target,
            send_sem=sent,
            recv_sem=received,
            device_id=device,
            device_id_type=MESH,
        )

    used = [0]

    def copy(source, target, device):
        number = used[0]
        used[0] += 1
        return between(source, target, device, send_sem.at[number], recv_sem.at[number])

    def local(source, target, number):
        return pltpu.make_async_copy(source, target, local_sem.at[number])

    def block(index):
        return pl.ds(pl.multiple_of(index * share, share), share)

    def piece_of(index, piece):
        return pl.ds(pl.multiple_of(index * share + piece * half, half), half)

    def strip(tile):
        return pl.ds(pl.multiple_of(tile * STRIP, STRIP), STRIP)

    def outgoing_image(number, owner, add):
        def shorten(tile, _):
            here = pl.ds(pl.multiple_of(owner * share + tile * STRIP, STRIP), STRIP)
            value = image_dir[here, :]
            if add:
                value = value + reduce_in[0, strip(tile), :].astype(F32)
            reduce_out[number, strip(tile), :] = value.astype(BF16)
            return 0

        lax.fori_loop(0, share // STRIP, shorten, 0)

    scale = scale_ref[0]
    bias = bias_ref[0]

    barrier = pltpu.get_barrier_semaphore()
    if stop == 16:
        met = [place[0], near_dp, side_dp]
    elif stop == 8:
        met = [place[0], near_dp, side_dp, near_far, side_far]
    else:
        met = place
    everyone = mates[1:] + [across] + [(index, slot) for index in met]
    for device in everyone:
        pl.semaphore_signal(barrier, inc=1, device_id=device, device_id_type=MESH)

    own_proj = local(projection_hbm, proj.at[pl.ds(0, part), :], 0)
    own_feature = local(
        feature_hbm.at[:, block(slot)], feature_rows.at[0, pl.ds(0, part), :], 1
    )
    own_image = local(image_hbm, image_ref, 2)
    for c in (own_feature, own_proj, own_image):
        c.start()
    pl.semaphore_wait(barrier, len(everyone))

    def text_copy(r, i):
        device = place[0] + r * (2 - r) * (place[1] - place[0])
        device = device + r * (r - 1) // 2 * (place[2] - place[0])
        rows_at = pl.ds(i * part, part)
        return between(
            feature_hbm.at[:, block(slot)] if i == 0 else feature_rows.at[0, rows_at, :],
            feature_rows.at[r + 1, rows_at, :],
            (device, slot),
            text_send.at[r * 4 + i],
            text_recv.at[r * 4 + i],
        )

    features = [None] * 4
    for i in (2, 3, 1):
        features[i] = copy(
            feature_hbm.at[:, block(peer[i])],
            feature_rows.at[0, pl.ds(i * part, part), :],
            mates[i],
        )
        features[i].start()
    def lanes(which):
        return pl.ds(pl.multiple_of(which * half, half), half)

    def rows_of(i):
        return pl.ds(i * part, part)

    def own_rows(i, which):
        if i == 0:
            return feature_hbm.at[:, piece_of(slot, which)]
        return feature_rows.at[0, rows_of(i), lanes(which)]

    near_half, side_half, near_on, side_on = [], [], [], []
    if stop:
        for i in range(4):
            near_half.append(
                copy(
                    own_rows(i, bit), feature_rows.at[3, rows_of(i), lanes(bit)], (near_dp, slot)
                )
            )
            side_half.append(copy(own_rows(i, 1 - bit), passing.at[rows_of(i), :], (side_dp, slot)))
            near_on.append(
                copy(
                    feature_rows.at[3, rows_of(i), lanes(1 - bit)],
                    feature_rows.at[2, rows_of(i), lanes(1 - bit)],
                    (near_far, slot),
                )
            )
            side_on.append(
                copy(
                    passing.at[rows_of(i), :],
                    feature_rows.at[2, rows_of(i), lanes(bit)],
                    (side_far, slot),
                )
            )
        near_rest = copy(
            feature_rows.at[0, :, lanes(1 - bit)],
            feature_rows.at[3, :, lanes(1 - bit)],
            (near_dp, slot),
        )

    def first_leg(i):
        if stop:
            near_half[i].start()
            side_half[i].start()
        for r in urgent:
            text_copy(r, i).start()

    def second_leg(i):
        near_half[i].wait_recv()
        near_on[i].start()
        side_half[i].wait_recv()
        side_on[i].start()

    first_leg(0)
    cut = part // 18 * 5
    rest = part - cut
    proj_wrap = copy(
        projection_hbm.at[pl.ds(cut, rest), :], proj.at[pl.ds(2 * part + cut, rest), :], across
    )
    proj_core = copy(projection_hbm, proj.at[pl.ds(part, part), :], mates[1])
    proj_near = copy(
        projection_hbm.at[pl.ds(0, cut), :], proj.at[pl.ds(2 * part, cut), :], mates[2]
    )
    proj_wrap.start()
    proj_core.start()

    def grad_copy(r, piece):
        at = pl.ds(pl.multiple_of(piece * half, half), half)
        device = place[0] + r * (2 - r) * (place[1] - place[0])
        device = device + r * (r - 1) // 2 * (place[2] - place[0])
        return between(
            grad_out.at[r, at, :],
            grad_in.at[r, at, :],
            (device, slot),
            grad_send.at[r * 2 + piece],
            grad_recv.at[r * 2 + piece],
        )

    def block_copy(i, turn):
        at = pl.ds(pl.multiple_of(turn * half, half), half)
        return between(
            block_out.at[i - 1, :, at],
            block_in.at[i - 1, :, at],
            mates[i],
            block_send.at[(i - 1) * 2 + turn],
            block_recv.at[(i - 1) * 2 + turn],
        )

    for i in (1, 2, 3):
        features[i].wait_recv()
        first_leg(i)
    proj_near.start()
    own_feature.wait()

    own_image.wait()

    def normalize(tile, _):
        at = strip(tile)
        wide = image_ref[at, :].astype(F32)
        image_low[at, :] = (wide * inverse_norm(wide)).astype(BF16)
        image_dir[at, :] = jnp.zeros((STRIP, width), F32)
        return 0

    lax.fori_loop(0, rows // STRIP, normalize, 0)

    proj_wrap.wait_recv()
    pass_wrap = copy(
        proj.at[pl.ds(2 * part + cut, rest), :],
        proj.at[pl.ds(3 * part + cut, rest), :],
        mates[1],
    )
    pass_wrap.start()
    proj_near.wait_recv()
    pass_near = copy(
        proj.at[pl.ds(2 * part, cut), :], proj.at[pl.ds(3 * part, cut), :], mates[1]
    )
    pass_near.start()
    own_proj.wait()
    proj_core.wait_recv()
    pass_wrap.wait_recv()
    pass_near.wait_recv()
    for r in late:
        for i in range(4):
            text_copy(r, i).start()
    if stop:
        for i in range(4):
            second_leg(i)
        near_rest.start()

    if stop:
        near_back = copy(
            grad_out.at[1, lanes(bit), :], relay_in.at[0], (near_far, slot)
        )
        side_back = copy(
            grad_out.at[1, lanes(1 - bit), :], relay_in.at[1], (side_far, slot)
        )
        near_direct = copy(
            grad_out.at[2, lanes(bit), :], grad_in.at[2, lanes(bit), :], (near_dp, slot)
        )
        near_sum = copy(relay_out, grad_in.at[2, lanes(1 - bit), :], (near_dp, slot))
        side_passed = copy(relay_in.at[1], grad_in.at[1, lanes(bit), :], (side_dp, slot))

    def window(unit, _):
        other = (unit + 3) // 4

        if stop:

            @pl.when(unit == 1)
            def _():
                for i in range(4):
                    text_copy(0, i).wait_recv()

            @pl.when(unit == 2)
            def _():
                for i in range(4):
                    near_on[i].wait_recv()
                    side_on[i].wait_recv()

            @pl.when(unit == 3)
            def _():
                near_rest.wait_recv()

        else:

            @pl.when(unit > 0)
            def _():
                for i in range(4):
                    text_copy(unit - 1, i).wait_recv()

        raw = lax.dot_general(
            feature_rows[unit], proj[...], FIRST, preferred_element_type=F32
        )
        text_raw[other] = raw

        def unit_text(tile, _):
            at = strip(tile)
            wide = text_raw[other, at, :]
            text_low[at, :] = (wide * inverse_norm(wide)).astype(BF16)
            text_dir[other, at, :] = jnp.zeros((STRIP, width), F32)
            return 0

        lax.fori_loop(0, share // STRIP, unit_text, 0)

        def step(tile, _):
            images = block(tile)
            image = image_low[images, :]
            text = text_low[...]
            logits = scale * lax.dot_general(image, text, LAST, preferred_element_type=F32) + bias
            line = lax.broadcasted_iota(jnp.int32, logits.shape, 0)
            column = lax.broadcasted_iota(jnp.int32, logits.shape, 1)
            same = line - column == (slot - tile) * share - unit * 4 * rows
            value = scale / (1.0 + jnp.exp(jnp.where(same, logits, -logits)))
            coeffs = jnp.where(same, -value, value).astype(BF16)
            image_dir[images, :] += jnp.dot(coeffs, text, preferred_element_type=F32)
            text_dir[other] += lax.dot_general(coeffs, image, FIRST, preferred_element_type=F32)
            return 0

        lax.fori_loop(0, rows // share, step, 0)

        @pl.when(unit > 0)
        def _():
            def shorten(tile, _):
                grad_out[unit - 1, strip(tile), :] = text_dir[1, strip(tile), :].astype(BF16)
                return 0

            lax.fori_loop(0, share // STRIP, shorten, 0)
            if not stop:
                grad_copy(unit - 1, 0).start()
                grad_copy(unit - 1, 1).start()

        if stop:

            @pl.when(unit == 1)
            def _():
                grad_copy(0, 0).start()
                grad_copy(0, 1).start()

            @pl.when(unit == 2)
            def _():
                near_back.start()
                side_back.start()

            @pl.when(unit == 3)
            def _():
                near_direct.start()

        return 0

    lax.fori_loop(0, 4, window, 0)

    outgoing_image(0, peer[3], False)
    reduce_far = copy(reduce_out.at[0], reduce_in.at[0], mates[1])
    reduce_far.start()
    outgoing_image(1, peer[1], False)
    reduce_core = copy(reduce_out.at[1], reduce_in.at[1], mates[1])
    reduce_core.start()
    reduce_far.wait_recv()
    outgoing_image(2, peer[2], True)
    reduce_cross = copy(reduce_out.at[2], reduce_in.at[2], mates[2])
    reduce_cross.start()

    if stop:
        side_back.wait_recv()
        side_passed.start()
        near_back.wait_recv()

        def add_on(tile, _):
            at = strip(tile)
            here = pl.ds(pl.multiple_of((1 - bit) * half + tile * STRIP, STRIP), STRIP)
            relay_out[at, :] = (text_dir[1, here, :] + relay_in[0, at, :].astype(F32)).astype(BF16)
            grad_in[1, pl.ds(pl.multiple_of(bit * half + tile * STRIP, STRIP), STRIP), :] = (
                jnp.zeros((STRIP, width), BF16)
            )
            return 0

        lax.fori_loop(0, half // STRIP, add_on, 0)
        near_sum.start()

    reduce_core.wait_recv()
    reduce_cross.wait_recv()

    def finish_image(tile, _):
        at = strip(tile)
        here = pl.ds(pl.multiple_of(slot * share + tile * STRIP, STRIP), STRIP)
        wide = image_ref[here, :].astype(F32)
        scaled = inverse_norm(wide)
        unit = wide * scaled
        total = image_dir[here, :] + reduce_in[1, at, :].astype(F32)
        total = total + reduce_in[2, at, :].astype(F32)
        total = total - unit * jnp.sum(unit * total, axis=1, keepdims=True)
        image_grad_ref[at, :] = total * scaled
        return 0

    lax.fori_loop(0, share // STRIP, finish_image, 0)

    def piece_in(turn):
        return turn * bit + (1 - turn) * (1 - bit) if stop else turn

    def finish_text(turn, _):
        piece = piece_in(turn)
        at = pl.ds(pl.multiple_of(piece * half, half), half)
        if stop:

            @pl.when(turn == 0)
            def _():
                grad_copy(0, 0).wait_recv()
                grad_copy(0, 1).wait_recv()
                near_direct.wait_recv()
                side_passed.wait_recv()

            @pl.when(turn == 1)
            def _():
                near_sum.wait_recv()

        else:
            for r in range(3):
                grad_copy(r, piece).wait_recv()

        def rows_done(tile, _):
            here = pl.ds(pl.multiple_of(piece * half + tile * STRIP, STRIP), STRIP)
            raw = text_raw[0, here, :]
            scaled = inverse_norm(raw)
            unit = raw * scaled
            total = text_dir[0, here, :] + grad_in[0, here, :].astype(F32)
            total = total + grad_in[1, here, :].astype(F32) + grad_in[2, here, :].astype(F32)
            total = total - unit * jnp.sum(unit * total, axis=1, keepdims=True)
            text_grad_ref[here, :] = total * scaled
            return 0

        lax.fori_loop(0, half // STRIP, rows_done, 0)
        values = lax.dot_general(
            proj[...], text_grad_ref[at, :].astype(BF16), LAST, preferred_element_type=F32
        )
        for i in (2, 3, 1):
            block_out[i - 1, :, lanes(turn)] = values[i * part : (i + 1) * part].astype(BF16)
            block_copy(i, turn).start()
        feature_grad_ref[:, piece_of(slot, piece)] = values[:part]
        return 0

    lax.fori_loop(0, 2, finish_text, 0)

    for turn in range(2):
        for i in (1, 2, 3):
            block_copy(i, turn).wait_recv()
            feature_grad_ref[:, piece_of(peer[i], piece_in(turn))] = block_in[
                i - 1, :, pl.ds(turn * half, half)
            ].astype(F32)

    for i in (1, 2, 3):
        features[i].wait_send()
        for piece in range(2):
            block_copy(i, piece).wait_send()
    for r in range(1 if stop else 3):
        for i in range(4):
            text_copy(r, i).wait_send()
        for piece in range(2):
            grad_copy(r, piece).wait_send()
    if stop:
        for c in near_half + side_half + near_on + side_on:
            c.wait_send()
        for c in (near_rest, near_back, side_back, near_direct, near_sum, side_passed):
            c.wait_send()
    for c in (proj_core, proj_near, proj_wrap, pass_near, pass_wrap):
        c.wait_send()
    for c in (reduce_far, reduce_core, reduce_cross):
        c.wait_send()


def fused(number, near, scale, bias, image, feature, projection):
    rows, width = image.shape
    part = feature.shape[0]
    share = rows // 4
    vmem = pl.BlockSpec(memory_space=pltpu.VMEM)
    smem = pl.BlockSpec(memory_space=pltpu.SMEM)
    any_space = pl.BlockSpec(memory_space=pl.ANY)
    semaphores = [36, 36, 12, 12, 6, 6, 6, 6, 3]
    return pl.pallas_call(
        functools.partial(kernel, near),
        out_shape=(
            jax.ShapeDtypeStruct((share, width), F32),
            jax.ShapeDtypeStruct((share, width), F32),
            jax.ShapeDtypeStruct((part, rows), F32),
        ),
        in_specs=[smem, smem, any_space, any_space, any_space],
        out_specs=[vmem, vmem, vmem],
        scratch_shapes=[
            pltpu.VMEM((rows, width), BF16),
            pltpu.VMEM((rows, width), BF16),
            pltpu.VMEM((4 * part, width), BF16),
            pltpu.VMEM((4, 4 * part, share), BF16),
            pltpu.VMEM((2, share, width), F32),
            pltpu.VMEM((share, width), BF16),
            pltpu.VMEM((rows, width), F32),
            pltpu.VMEM((2, share, width), F32),
            pltpu.VMEM((3, share, width), BF16),
            pltpu.VMEM((3, share, width), BF16),
            pltpu.VMEM((3, share, width), BF16),
            pltpu.VMEM((3, share, width), BF16),
            pltpu.VMEM((3, part, share), BF16),
            pltpu.VMEM((3, part, share), BF16),
            pltpu.VMEM((4 * part, share // 2), BF16),
            pltpu.VMEM((2, share // 2, width), BF16),
            pltpu.VMEM((share // 2, width), BF16),
        ]
        + [pltpu.SemaphoreType.DMA((count,)) for count in semaphores],
        compiler_params=pltpu.CompilerParams(
            collective_id=number, has_side_effects=True, vmem_limit_bytes=56 * 1024 * 1024
        ),
    )(scale, bias, image, feature, projection)


def per_device(image_embed, text_feature, projection, logit_scale, logit_bias, partner_masks):
    chosen = partner_masks[0] + partner_masks[1] + partner_masks[2] - FAR
    which = jnp.int32(0)
    for number, pair in enumerate(PAIRS):
        which = jnp.where(chosen == sum(pair), number, which)
    image_grad, text_grad, feature_grad = lax.switch(
        which,
        [functools.partial(fused, number, pair) for number, pair in enumerate(PAIRS)],
        logit_scale,
        logit_bias,
        image_embed,
        text_feature.T,
        projection,
    )
    return (image_grad, text_grad, feature_grad.T)


def solution(mesh):
    return jax.shard_map(
        per_device,
        mesh=mesh,
        in_specs=(P("dp", None), P("dp", "tensor"), P("tensor", None), P(), P(), P()),
        out_specs=(P(("dp", "tensor"), None), P(("dp", "tensor"), None), P("dp", "tensor")),
        check_vma=False,
    )
```

```python
import functools

import jax
import jax.numpy as jnp
from jax import lax
from jax.experimental import pallas as pl
from jax.experimental.pallas import tpu as pltpu
from jax.sharding import PartitionSpec as P

EPSILON = 1e-06
MESH = pl.DeviceIdType.MESH
FAR = 32
STRIP = 64
CLOSE = (1, 2, 4)
PAIRS = ((1, 2), (1, 4), (2, 4), (0, 8), (0, 16), (8, 16))
F32 = jnp.float32
BF16 = jnp.bfloat16
LAST = (((1,), (1,)), ((), ()))
FIRST = (((0,), (0,)), ((), ()))


def flipped(index, bit):
    return index + bit - 2 * bit * (index // bit % 2)


def stop_of(near):
    return 16 if 16 in near else 8 if 8 in near else 0


def order_of(near):
    stop = stop_of(near)
    if stop:
        return tuple(mask for mask in near if mask != stop) + (FAR, stop)
    if 4 in near:
        return (FAR, 4) + tuple(mask for mask in near if mask != 4)
    return (near[0], FAR, near[1])


def inverse_norm(values):
    return 1.0 / jnp.sqrt(jnp.sum(values * values, axis=1, keepdims=True) + EPSILON)


def kernel(
    near,
    scale_ref,
    bias_ref,
    mask_ref,
    image_hbm,
    feature_hbm,
    projection_hbm,
    image_grad_ref,
    text_grad_ref,
    feature_grad_ref,
    image_ref,
    image_low,
    proj,
    feature_rows,
    text_raw,
    text_low,
    image_dir,
    text_dir,
    grad_out,
    grad_in,
    reduce_out,
    reduce_in,
    block_out,
    block_in,
    passing,
    relay_in,
    relay_out,
    close_rows,
    close_in,
    send_sem,
    recv_sem,
    text_send,
    text_recv,
    grad_send,
    grad_recv,
    block_send,
    block_recv,
    local_sem,
):
    rows, width = image_ref.shape
    part = feature_hbm.shape[0]
    share = rows // 4
    half = share // 2
    dp = lax.axis_index("dp")
    slot = lax.axis_index("tensor")
    core = slot % 2
    side = slot // 2
    peer = [
        slot,
        2 * side + 1 - core,
        2 * (1 - side) + core,
        2 * (1 - side) + 1 - core,
    ]
    turns = order_of(near)
    place = [flipped(dp, mask) if mask else dp for mask in turns]
    merged = turns[0] == 0
    close = [flipped(dp, mask) for mask in CLOSE]
    stop = stop_of(near)
    urgent = [] if merged else [0] if stop else [r for r in range(3) if turns[r] != 4]
    late = [r for r in range(3) if turns[r] == 4]
    bit = dp // max(stop, 1) % 2
    near_dp = place[2]
    side_dp = lax.rem(dp + 64 + stop * (2 * bit - 1), 64)
    near_far, side_far = flipped(near_dp, FAR), flipped(side_dp, FAR)
    across = (flipped(dp, 4), peer[2])
    mates = [(dp, peer[i]) for i in range(4)]

    def between(source, target, device, sent, received):
        return pltpu.make_async_remote_copy(
            src_ref=source,
            dst_ref=target,
            send_sem=sent,
            recv_sem=received,
            device_id=device,
            device_id_type=MESH,
        )

    used = [0]

    def copy(source, target, device):
        number = used[0]
        used[0] += 1
        return between(source, target, device, send_sem.at[number], recv_sem.at[number])

    def local(source, target, number):
        return pltpu.make_async_copy(source, target, local_sem.at[number])

    def block(index):
        return pl.ds(pl.multiple_of(index * share, share), share)

    def piece_of(index, piece):
        return pl.ds(pl.multiple_of(index * share + piece * half, half), half)

    def strip(tile):
        return pl.ds(pl.multiple_of(tile * STRIP, STRIP), STRIP)

    def outgoing_image(number, owner, add):
        def shorten(tile, _):
            here = pl.ds(pl.multiple_of(owner * share + tile * STRIP, STRIP), STRIP)
            value = image_dir[here, :]
            if add:
                value = value + reduce_in[0, strip(tile), :].astype(F32)
            reduce_out[number, strip(tile), :] = value.astype(BF16)
            return 0

        lax.fori_loop(0, share // STRIP, shorten, 0)

    def choice():
        close_sum = sum(jnp.where(mask_ref[i] < 8, mask_ref[i], 0) for i in range(3))
        return jnp.minimum(close_sum // 2, 2)

    scale = scale_ref[0]
    bias = bias_ref[0]

    barrier = pltpu.get_barrier_semaphore()
    if stop:
        met = close if merged else place[:1]
        met = met + [near_dp, side_dp] + ([near_far, side_far] if stop == 8 else [])
    else:
        met = place
    everyone = mates[1:] + [across] + [(index, slot) for index in met]
    for device in everyone:
        pl.semaphore_signal(barrier, inc=1, device_id=device, device_id_type=MESH)

    own_proj = local(projection_hbm, proj.at[pl.ds(0, part), :], 0)
    own_feature = local(
        feature_hbm.at[:, block(slot)], feature_rows.at[0, pl.ds(0, part), :], 1
    )
    own_image = local(image_hbm, image_ref, 2)
    for c in (own_feature, own_proj, own_image):
        c.start()
    pl.semaphore_wait(barrier, len(everyone))

    def text_copy(r, i):
        device = place[0] + r * (2 - r) * (place[1] - place[0])
        device = device + r * (r - 1) // 2 * (place[2] - place[0])
        rows_at = pl.ds(i * part, part)
        return between(
            feature_hbm.at[:, block(slot)] if i == 0 else feature_rows.at[0, rows_at, :],
            feature_rows.at[r + 1, rows_at, :],
            (device, slot),
            text_send.at[r * 4 + i],
            text_recv.at[r * 4 + i],
        )

    features = [None] * 4
    for i in (2, 3, 1):
        features[i] = copy(
            feature_hbm.at[:, block(peer[i])],
            feature_rows.at[0, pl.ds(i * part, part), :],
            mates[i],
        )
        features[i].start()
    def close_text(m, i):
        source = feature_hbm.at[:, block(slot)]
        if i:
            source = feature_rows.at[0, pl.ds(i * part, part), :]
        return between(
            source,
            close_rows.at[m, pl.ds(i * part, part), :],
            (close[m], slot),
            text_send.at[m * 4 + i],
            text_recv.at[m * 4 + i],
        )

    def close_grad(m, piece):
        at = pl.ds(piece * half, half)
        return between(
            grad_out.at[0, at, :],
            close_in.at[m, at, :],
            (close[m], slot),
            grad_send.at[m * 2 + piece],
            grad_recv.at[m * 2 + piece],
        )

    def lanes(which):
        return pl.ds(pl.multiple_of(which * half, half), half)

    def rows_of(i):
        return pl.ds(i * part, part)

    def own_rows(i, which):
        if i == 0:
            return feature_hbm.at[:, piece_of(slot, which)]
        return feature_rows.at[0, rows_of(i), lanes(which)]

    near_half, side_half, near_on, side_on = [], [], [], []
    if stop:
        for i in range(4):
            near_half.append(
                copy(
                    own_rows(i, bit), feature_rows.at[3, rows_of(i), lanes(bit)], (near_dp, slot)
                )
            )
            side_half.append(copy(own_rows(i, 1 - bit), passing.at[rows_of(i), :], (side_dp, slot)))
            near_on.append(
                copy(
                    feature_rows.at[3, rows_of(i), lanes(1 - bit)],
                    feature_rows.at[2, rows_of(i), lanes(1 - bit)],
                    (near_far, slot),
                )
            )
            side_on.append(
                copy(
                    passing.at[rows_of(i), :],
                    feature_rows.at[2, rows_of(i), lanes(bit)],
                    (side_far, slot),
                )
            )
        near_rest = copy(
            feature_rows.at[0, :, lanes(1 - bit)],
            feature_rows.at[3, :, lanes(1 - bit)],
            (near_dp, slot),
        )

    def first_leg(i):
        if stop:
            near_half[i].start()
            side_half[i].start()
        for r in urgent:
            text_copy(r, i).start()
        if merged:
            for m in range(2):
                close_text(m, i).start()

    def second_leg(i):
        near_half[i].wait_recv()
        near_on[i].start()
        side_half[i].wait_recv()
        side_on[i].start()

    first_leg(0)
    cut = part // 18 * 5
    rest = part - cut
    proj_wrap = copy(
        projection_hbm.at[pl.ds(cut, rest), :], proj.at[pl.ds(2 * part + cut, rest), :], across
    )
    proj_core = copy(projection_hbm, proj.at[pl.ds(part, part), :], mates[1])
    proj_near = copy(
        projection_hbm.at[pl.ds(0, cut), :], proj.at[pl.ds(2 * part, cut), :], mates[2]
    )
    proj_wrap.start()
    proj_core.start()

    def grad_copy(r, piece):
        at = pl.ds(pl.multiple_of(piece * half, half), half)
        device = place[0] + r * (2 - r) * (place[1] - place[0])
        device = device + r * (r - 1) // 2 * (place[2] - place[0])
        return between(
            grad_out.at[r, at, :],
            grad_in.at[r, at, :],
            (device, slot),
            grad_send.at[r * 2 + piece],
            grad_recv.at[r * 2 + piece],
        )

    def block_copy(i, turn):
        at = pl.ds(pl.multiple_of(turn * half, half), half)
        return between(
            block_out.at[i - 1, :, at],
            block_in.at[i - 1, :, at],
            mates[i],
            block_send.at[(i - 1) * 2 + turn],
            block_recv.at[(i - 1) * 2 + turn],
        )

    for i in (1, 2, 3):
        features[i].wait_recv()
        first_leg(i)
    proj_near.start()
    own_feature.wait()

    own_image.wait()

    def normalize(tile, _):
        at = strip(tile)
        wide = image_ref[at, :].astype(F32)
        image_low[at, :] = (wide * inverse_norm(wide)).astype(BF16)
        image_dir[at, :] = jnp.zeros((STRIP, width), F32)
        return 0

    lax.fori_loop(0, rows // STRIP, normalize, 0)

    proj_wrap.wait_recv()
    pass_wrap = copy(
        proj.at[pl.ds(2 * part + cut, rest), :],
        proj.at[pl.ds(3 * part + cut, rest), :],
        mates[1],
    )
    pass_wrap.start()
    proj_near.wait_recv()
    pass_near = copy(
        proj.at[pl.ds(2 * part, cut), :], proj.at[pl.ds(3 * part, cut), :], mates[1]
    )
    pass_near.start()
    own_proj.wait()
    proj_core.wait_recv()
    pass_wrap.wait_recv()
    pass_near.wait_recv()
    for i in range(4):
        for r in late:
            text_copy(r, i).start()
        if merged:
            close_text(2, i).start()
    if stop:
        for i in range(4):
            second_leg(i)
        near_rest.start()

    if stop:
        near_back = copy(
            grad_out.at[1, lanes(bit), :], relay_in.at[0], (near_far, slot)
        )
        side_back = copy(
            grad_out.at[1, lanes(1 - bit), :], relay_in.at[1], (side_far, slot)
        )
        near_direct = copy(
            grad_out.at[2, lanes(bit), :], grad_in.at[2, lanes(bit), :], (near_dp, slot)
        )
        near_sum = copy(relay_out, grad_in.at[2, lanes(1 - bit), :], (near_dp, slot))
        side_passed = copy(relay_in.at[1], grad_in.at[1, lanes(bit), :], (side_dp, slot))

    def window(unit, _):
        other = (unit + 3) // 4

        if stop:

            @pl.when(unit == 1)
            def _():
                if merged:
                    for m in range(3):
                        for i in range(4):
                            close_text(m, i).wait_recv()

                    def take(tile, _):
                        at = pl.ds(pl.multiple_of(tile * 96, 96), 96)
                        feature_rows[1, at, :] = close_rows[choice(), at, :]
                        return 0

                    lax.fori_loop(0, 4 * part // 96, take, 0)
                else:
                    for i in range(4):
                        text_copy(0, i).wait_recv()

            @pl.when(unit == 2)
            def _():
                for i in range(4):
                    near_on[i].wait_recv()
                    side_on[i].wait_recv()

            @pl.when(unit == 3)
            def _():
                near_rest.wait_recv()

        else:

            @pl.when(unit > 0)
            def _():
                for i in range(4):
                    text_copy(unit - 1, i).wait_recv()

        raw = lax.dot_general(
            feature_rows[unit], proj[...], FIRST, preferred_element_type=F32
        )
        text_raw[other] = raw

        def unit_text(tile, _):
            at = strip(tile)
            wide = text_raw[other, at, :]
            text_low[at, :] = (wide * inverse_norm(wide)).astype(BF16)
            text_dir[other, at, :] = jnp.zeros((STRIP, width), F32)
            return 0

        lax.fori_loop(0, share // STRIP, unit_text, 0)

        def step(tile, _):
            images = block(tile)
            image = image_low[images, :]
            text = text_low[...]
            logits = scale * lax.dot_general(image, text, LAST, preferred_element_type=F32) + bias
            line = lax.broadcasted_iota(jnp.int32, logits.shape, 0)
            column = lax.broadcasted_iota(jnp.int32, logits.shape, 1)
            same = line - column == (slot - tile) * share - unit * 4 * rows
            value = scale / (1.0 + jnp.exp(jnp.where(same, logits, -logits)))
            coeffs = jnp.where(same, -value, value).astype(BF16)
            image_dir[images, :] += jnp.dot(coeffs, text, preferred_element_type=F32)
            text_dir[other] += lax.dot_general(coeffs, image, FIRST, preferred_element_type=F32)
            return 0

        lax.fori_loop(0, rows // share, step, 0)

        @pl.when(unit > 0)
        def _():
            def shorten(tile, _):
                grad_out[unit - 1, strip(tile), :] = text_dir[1, strip(tile), :].astype(BF16)
                return 0

            lax.fori_loop(0, share // STRIP, shorten, 0)
            if not stop:
                grad_copy(unit - 1, 0).start()
                grad_copy(unit - 1, 1).start()

        if stop:

            @pl.when(unit == 1)
            def _():
                for piece in range(2):
                    if merged:
                        for m in range(3):
                            close_grad(m, piece).start()
                    else:
                        grad_copy(0, piece).start()

            @pl.when(unit == 2)
            def _():
                near_back.start()
                side_back.start()

            @pl.when(unit == 3)
            def _():
                near_direct.start()

        return 0

    lax.fori_loop(0, 4, window, 0)

    outgoing_image(0, peer[3], False)
    reduce_far = copy(reduce_out.at[0], reduce_in.at[0], mates[1])
    reduce_far.start()
    outgoing_image(1, peer[1], False)
    reduce_core = copy(reduce_out.at[1], reduce_in.at[1], mates[1])
    reduce_core.start()
    reduce_far.wait_recv()
    outgoing_image(2, peer[2], True)
    reduce_cross = copy(reduce_out.at[2], reduce_in.at[2], mates[2])
    reduce_cross.start()

    if stop:
        side_back.wait_recv()
        side_passed.start()
        near_back.wait_recv()

        def add_on(tile, _):
            at = strip(tile)
            here = pl.ds(pl.multiple_of((1 - bit) * half + tile * STRIP, STRIP), STRIP)
            relay_out[at, :] = (text_dir[1, here, :] + relay_in[0, at, :].astype(F32)).astype(BF16)
            grad_in[1, pl.ds(pl.multiple_of(bit * half + tile * STRIP, STRIP), STRIP), :] = (
                jnp.zeros((STRIP, width), BF16)
            )
            return 0

        lax.fori_loop(0, half // STRIP, add_on, 0)
        near_sum.start()

    reduce_core.wait_recv()
    reduce_cross.wait_recv()

    def finish_image(tile, _):
        at = strip(tile)
        here = pl.ds(pl.multiple_of(slot * share + tile * STRIP, STRIP), STRIP)
        wide = image_ref[here, :].astype(F32)
        scaled = inverse_norm(wide)
        unit = wide * scaled
        total = image_dir[here, :] + reduce_in[1, at, :].astype(F32)
        total = total + reduce_in[2, at, :].astype(F32)
        total = total - unit * jnp.sum(unit * total, axis=1, keepdims=True)
        image_grad_ref[at, :] = total * scaled
        return 0

    lax.fori_loop(0, share // STRIP, finish_image, 0)

    def piece_in(turn):
        return turn * bit + (1 - turn) * (1 - bit) if stop else turn

    def finish_text(turn, _):
        piece = piece_in(turn)
        at = pl.ds(pl.multiple_of(piece * half, half), half)
        if stop:

            @pl.when(turn == 0)
            def _():
                for part_of in range(2):
                    if merged:
                        for m in range(3):
                            close_grad(m, part_of).wait_recv()
                    else:
                        grad_copy(0, part_of).wait_recv()
                near_direct.wait_recv()
                side_passed.wait_recv()

            @pl.when(turn == 1)
            def _():
                near_sum.wait_recv()

        else:
            for r in range(3):
                grad_copy(r, piece).wait_recv()

        def rows_done(tile, _):
            here = pl.ds(pl.multiple_of(piece * half + tile * STRIP, STRIP), STRIP)
            raw = text_raw[0, here, :]
            scaled = inverse_norm(raw)
            unit = raw * scaled
            first = close_in[choice(), here, :] if merged else grad_in[0, here, :]
            total = text_dir[0, here, :] + first.astype(F32)
            total = total + grad_in[1, here, :].astype(F32) + grad_in[2, here, :].astype(F32)
            total = total - unit * jnp.sum(unit * total, axis=1, keepdims=True)
            text_grad_ref[here, :] = total * scaled
            return 0

        lax.fori_loop(0, half // STRIP, rows_done, 0)
        values = lax.dot_general(
            proj[...], text_grad_ref[at, :].astype(BF16), LAST, preferred_element_type=F32
        )
        for i in (2, 3, 1):
            block_out[i - 1, :, lanes(turn)] = values[i * part : (i + 1) * part].astype(BF16)
            block_copy(i, turn).start()
        feature_grad_ref[:, piece_of(slot, piece)] = values[:part]
        return 0

    lax.fori_loop(0, 2, finish_text, 0)

    for turn in range(2):
        for i in (1, 2, 3):
            block_copy(i, turn).wait_recv()
            feature_grad_ref[:, piece_of(peer[i], piece_in(turn))] = block_in[
                i - 1, :, pl.ds(turn * half, half)
            ].astype(F32)

    for i in (1, 2, 3):
        features[i].wait_send()
        for piece in range(2):
            block_copy(i, piece).wait_send()
    if merged:
        for m in range(3):
            for i in range(4):
                close_text(m, i).wait_send()
            for piece in range(2):
                close_grad(m, piece).wait_send()
    for r in range(0 if merged else 1 if stop else 3):
        for i in range(4):
            text_copy(r, i).wait_send()
        for piece in range(2):
            grad_copy(r, piece).wait_send()
    if stop:
        for c in near_half + side_half + near_on + side_on:
            c.wait_send()
        for c in (near_rest, near_back, side_back, near_direct, near_sum, side_passed):
            c.wait_send()
    for c in (proj_core, proj_near, proj_wrap, pass_near, pass_wrap):
        c.wait_send()
    for c in (reduce_far, reduce_core, reduce_cross):
        c.wait_send()


def fused(number, near, scale, bias, masks, image, feature, projection):
    rows, width = image.shape
    part = feature.shape[0]
    share = rows // 4
    vmem = pl.BlockSpec(memory_space=pltpu.VMEM)
    smem = pl.BlockSpec(memory_space=pltpu.SMEM)
    any_space = pl.BlockSpec(memory_space=pl.ANY)
    semaphores = [36, 36, 12, 12, 6, 6, 6, 6, 3]
    return pl.pallas_call(
        functools.partial(kernel, near),
        out_shape=(
            jax.ShapeDtypeStruct((share, width), F32),
            jax.ShapeDtypeStruct((share, width), F32),
            jax.ShapeDtypeStruct((part, rows), F32),
        ),
        in_specs=[smem, smem, smem, any_space, any_space, any_space],
        out_specs=[vmem, vmem, vmem],
        scratch_shapes=[
            pltpu.VMEM((rows, width), BF16),
            pltpu.VMEM((rows, width), BF16),
            pltpu.VMEM((4 * part, width), BF16),
            pltpu.VMEM((4, 4 * part, share), BF16),
            pltpu.VMEM((2, share, width), F32),
            pltpu.VMEM((share, width), BF16),
            pltpu.VMEM((rows, width), F32),
            pltpu.VMEM((2, share, width), F32),
            pltpu.VMEM((3, share, width), BF16),
            pltpu.VMEM((3, share, width), BF16),
            pltpu.VMEM((3, share, width), BF16),
            pltpu.VMEM((3, share, width), BF16),
            pltpu.VMEM((3, part, share), BF16),
            pltpu.VMEM((3, part, share), BF16),
            pltpu.VMEM((4 * part, share // 2), BF16),
            pltpu.VMEM((2, share // 2, width), BF16),
            pltpu.VMEM((share // 2, width), BF16),
            pltpu.VMEM((3, 4 * part, share), BF16),
            pltpu.VMEM((3, share, width), BF16),
        ]
        + [pltpu.SemaphoreType.DMA((count,)) for count in semaphores],
        compiler_params=pltpu.CompilerParams(
            collective_id=number, has_side_effects=True, vmem_limit_bytes=56 * 1024 * 1024
        ),
    )(scale, bias, masks, image, feature, projection)


def per_device(image_embed, text_feature, projection, logit_scale, logit_bias, partner_masks):
    chosen = partner_masks[0] + partner_masks[1] + partner_masks[2] - FAR
    which = jnp.where(chosen == 24, 5, jnp.where(chosen > 16, 4, 3))
    which = jnp.where(chosen < 8, (chosen - 2) // 2, which)
    image_grad, text_grad, feature_grad = lax.switch(
        which,
        [functools.partial(fused, number, pair) for number, pair in enumerate(PAIRS)],
        logit_scale,
        logit_bias,
        partner_masks,
        image_embed,
        text_feature.T,
        projection,
    )
    return (image_grad, text_grad, feature_grad.T)


def solution(mesh):
    return jax.shard_map(
        per_device,
        mesh=mesh,
        in_specs=(P("dp", None), P("dp", "tensor"), P("tensor", None), P(), P(), P()),
        out_specs=(P(("dp", "tensor"), None), P(("dp", "tensor"), None), P("dp", "tensor")),
        check_vma=False,
    )
```

```python
import functools

import jax
import jax.numpy as jnp
from jax import lax
from jax.experimental import pallas as pl
from jax.experimental.pallas import tpu as pltpu
from jax.sharding import PartitionSpec as P

EPSILON = 1e-06
MESH = pl.DeviceIdType.MESH
FAR = 32
STRIP = 64
CLOSE = (1, 2, 4)
PAIRS = ((1, 2), (1, 4), (2, 4), (0, 8), (0, 16), (8, 16))
F32 = jnp.float32
BF16 = jnp.bfloat16
LAST = (((1,), (1,)), ((), ()))
FIRST = (((0,), (0,)), ((), ()))


def flipped(index, bit):
    return index + bit - 2 * bit * (index // bit % 2)


def stop_of(near):
    return 16 if 16 in near else 8 if 8 in near else 0


def order_of(near):
    stop = stop_of(near)
    if stop:
        return tuple(mask for mask in near if mask != stop) + (FAR, stop)
    if 4 in near:
        return (FAR, 4) + tuple(mask for mask in near if mask != 4)
    return (near[0], FAR, near[1])


def inverse_norm(values):
    return 1.0 / jnp.sqrt(jnp.sum(values * values, axis=1, keepdims=True) + EPSILON)


def kernel(
    near,
    scale_ref,
    bias_ref,
    mask_ref,
    image_hbm,
    feature_hbm,
    projection_hbm,
    image_grad_ref,
    text_grad_ref,
    feature_grad_ref,
    image_ref,
    image_low,
    proj,
    feature_rows,
    text_raw,
    text_low,
    image_dir,
    text_dir,
    grad_out,
    grad_in,
    reduce_out,
    reduce_in,
    block_out,
    block_in,
    passing,
    relay_in,
    relay_out,
    close_rows,
    close_in,
    send_sem,
    recv_sem,
    text_send,
    text_recv,
    grad_send,
    grad_recv,
    block_send,
    block_recv,
    local_sem,
):
    rows, width = image_ref.shape
    part = feature_hbm.shape[0]
    share = rows // 4
    half = share // 2
    dp = lax.axis_index("dp")
    slot = lax.axis_index("tensor")
    core = slot % 2
    side = slot // 2
    peer = [
        slot,
        2 * side + 1 - core,
        2 * (1 - side) + core,
        2 * (1 - side) + 1 - core,
    ]
    turns = order_of(near)
    place = [flipped(dp, mask) if mask else dp for mask in turns]
    merged = turns[0] == 0
    close = [flipped(dp, mask) for mask in CLOSE]
    stop = stop_of(near)
    urgent = [] if merged else [0] if stop else [r for r in range(3) if turns[r] != 4]
    late = [r for r in range(3) if turns[r] == 4]
    bit = dp // max(stop, 1) % 2
    near_dp = place[2]
    side_dp = lax.rem(dp + 64 + stop * (2 * bit - 1), 64)
    near_far, side_far = flipped(near_dp, FAR), flipped(side_dp, FAR)
    across = (flipped(dp, 4), peer[2])
    mates = [(dp, peer[i]) for i in range(4)]

    def between(source, target, device, sent, received):
        return pltpu.make_async_remote_copy(
            src_ref=source,
            dst_ref=target,
            send_sem=sent,
            recv_sem=received,
            device_id=device,
            device_id_type=MESH,
        )

    used = [0]

    def copy(source, target, device):
        number = used[0]
        used[0] += 1
        return between(source, target, device, send_sem.at[number], recv_sem.at[number])

    def local(source, target, number):
        return pltpu.make_async_copy(source, target, local_sem.at[number])

    def block(index):
        return pl.ds(pl.multiple_of(index * share, share), share)

    def piece_of(index, piece):
        return pl.ds(pl.multiple_of(index * share + piece * half, half), half)

    def strip(tile):
        return pl.ds(pl.multiple_of(tile * STRIP, STRIP), STRIP)

    def outgoing_image(number, owner, add):
        def shorten(tile, _):
            here = pl.ds(pl.multiple_of(owner * share + tile * STRIP, STRIP), STRIP)
            value = image_dir[here, :]
            if add:
                value = value + reduce_in[0, strip(tile), :].astype(F32)
            reduce_out[number, strip(tile), :] = value.astype(BF16)
            return 0

        lax.fori_loop(0, share // STRIP, shorten, 0)

    def choice():
        close_sum = sum(jnp.where(mask_ref[i] < 8, mask_ref[i], 0) for i in range(3))
        return jnp.minimum(close_sum // 2, 2)

    scale = scale_ref[0]
    bias = bias_ref[0]

    barrier = pltpu.get_barrier_semaphore()
    if stop:
        met = close if merged else place[:1]
        met = met + [near_dp, side_dp] + ([near_far, side_far] if stop == 8 else [])
    else:
        met = place
    everyone = mates[1:] + [across] + [(index, slot) for index in met]
    for device in everyone:
        pl.semaphore_signal(barrier, inc=1, device_id=device, device_id_type=MESH)

    own_proj = local(projection_hbm, proj.at[pl.ds(0, part), :], 0)
    own_feature = local(
        feature_hbm.at[:, block(slot)], feature_rows.at[0, pl.ds(0, part), :], 1
    )
    own_image = local(image_hbm, image_ref, 2)
    for c in (own_feature, own_proj, own_image):
        c.start()
    pl.semaphore_wait(barrier, len(everyone))

    def text_copy(r, i):
        device = place[0] + r * (2 - r) * (place[1] - place[0])
        device = device + r * (r - 1) // 2 * (place[2] - place[0])
        rows_at = pl.ds(i * part, part)
        return between(
            feature_hbm.at[:, block(slot)] if i == 0 else feature_rows.at[0, rows_at, :],
            feature_rows.at[r + 1, rows_at, :],
            (device, slot),
            text_send.at[r * 4 + i],
            text_recv.at[r * 4 + i],
        )

    features = [None] * 4
    for i in (2, 3, 1):
        features[i] = copy(
            feature_hbm.at[:, block(peer[i])],
            feature_rows.at[0, pl.ds(i * part, part), :],
            mates[i],
        )
        features[i].start()
    def close_text(m, i):
        source = feature_hbm.at[:, block(slot)]
        if i:
            source = feature_rows.at[0, pl.ds(i * part, part), :]
        return between(
            source,
            close_rows.at[m, pl.ds(i * part, part), :],
            (close[m], slot),
            text_send.at[m * 4 + i],
            text_recv.at[m * 4 + i],
        )

    def close_grad(m, piece):
        at = pl.ds(piece * half, half)
        return between(
            grad_out.at[0, at, :],
            close_in.at[m, at, :],
            (close[m], slot),
            grad_send.at[m * 2 + piece],
            grad_recv.at[m * 2 + piece],
        )

    def lanes(which):
        return pl.ds(pl.multiple_of(which * half, half), half)

    def rows_of(i):
        return pl.ds(i * part, part)

    def own_rows(i, which):
        if i == 0:
            return feature_hbm.at[:, piece_of(slot, which)]
        return feature_rows.at[0, rows_of(i), lanes(which)]

    near_half, side_half, near_on, side_on = [], [], [], []
    if stop:
        for i in range(4):
            near_half.append(
                copy(
                    own_rows(i, bit), feature_rows.at[3, rows_of(i), lanes(bit)], (near_dp, slot)
                )
            )
            side_half.append(copy(own_rows(i, 1 - bit), passing.at[rows_of(i), :], (side_dp, slot)))
            near_on.append(
                copy(
                    feature_rows.at[3, rows_of(i), lanes(1 - bit)],
                    feature_rows.at[2, rows_of(i), lanes(1 - bit)],
                    (near_far, slot),
                )
            )
            side_on.append(
                copy(
                    passing.at[rows_of(i), :],
                    feature_rows.at[2, rows_of(i), lanes(bit)],
                    (side_far, slot),
                )
            )
        near_rest = copy(
            feature_rows.at[0, :, lanes(1 - bit)],
            feature_rows.at[3, :, lanes(1 - bit)],
            (near_dp, slot),
        )

    def first_leg(i):
        if stop:
            near_half[i].start()
            side_half[i].start()
        for r in urgent:
            text_copy(r, i).start()
        if merged:
            for m in range(2):
                close_text(m, i).start()

    def second_leg(i):
        near_half[i].wait_recv()
        near_on[i].start()
        side_half[i].wait_recv()
        side_on[i].start()

    first_leg(0)
    cut = part // 18 * 5
    rest = part - cut
    proj_wrap = copy(
        projection_hbm.at[pl.ds(cut, rest), :], proj.at[pl.ds(2 * part + cut, rest), :], across
    )
    proj_core = copy(projection_hbm, proj.at[pl.ds(part, part), :], mates[1])
    proj_near = copy(
        projection_hbm.at[pl.ds(0, cut), :], proj.at[pl.ds(2 * part, cut), :], mates[2]
    )
    proj_wrap.start()
    proj_core.start()

    def grad_copy(r, piece):
        at = pl.ds(pl.multiple_of(piece * half, half), half)
        device = place[0] + r * (2 - r) * (place[1] - place[0])
        device = device + r * (r - 1) // 2 * (place[2] - place[0])
        return between(
            grad_out.at[r, at, :],
            grad_in.at[r, at, :],
            (device, slot),
            grad_send.at[r * 2 + piece],
            grad_recv.at[r * 2 + piece],
        )

    def block_copy(i, turn):
        at = pl.ds(pl.multiple_of(turn * half, half), half)
        return between(
            block_out.at[i - 1, :, at],
            block_in.at[i - 1, :, at],
            mates[i],
            block_send.at[(i - 1) * 2 + turn],
            block_recv.at[(i - 1) * 2 + turn],
        )

    for i in (1, 2, 3):
        features[i].wait_recv()
        first_leg(i)
    proj_near.start()
    own_feature.wait()

    own_image.wait()

    def normalize(tile, _):
        at = strip(tile)
        wide = image_ref[at, :].astype(F32)
        image_low[at, :] = (wide * inverse_norm(wide)).astype(BF16)
        image_dir[at, :] = jnp.zeros((STRIP, width), F32)
        return 0

    lax.fori_loop(0, rows // STRIP, normalize, 0)

    proj_wrap.wait_recv()
    pass_wrap = copy(
        proj.at[pl.ds(2 * part + cut, rest), :],
        proj.at[pl.ds(3 * part + cut, rest), :],
        mates[1],
    )
    pass_wrap.start()
    proj_near.wait_recv()
    pass_near = copy(
        proj.at[pl.ds(2 * part, cut), :], proj.at[pl.ds(3 * part, cut), :], mates[1]
    )
    pass_near.start()
    own_proj.wait()
    proj_core.wait_recv()
    pass_wrap.wait_recv()
    pass_near.wait_recv()
    for i in range(4):
        for r in late:
            text_copy(r, i).start()
        if merged:
            close_text(2, i).start()
    if stop:
        for i in range(4):
            second_leg(i)
        near_rest.start()

    if stop:
        near_back = copy(
            grad_out.at[1, lanes(bit), :], relay_in.at[0], (near_far, slot)
        )
        side_back = copy(
            grad_out.at[1, lanes(1 - bit), :], relay_in.at[1], (side_far, slot)
        )
        near_direct = copy(
            grad_out.at[2, lanes(bit), :], grad_in.at[2, lanes(bit), :], (near_dp, slot)
        )
        near_sum = copy(relay_out, grad_in.at[2, lanes(1 - bit), :], (near_dp, slot))
        side_passed = copy(relay_in.at[1], grad_in.at[1, lanes(bit), :], (side_dp, slot))

    def window(unit, _):
        other = (unit + 3) // 4

        if stop:

            @pl.when(unit == 1)
            def _():
                if merged:
                    for m in range(3):
                        for i in range(4):
                            close_text(m, i).wait_recv()

                    def take(tile, _):
                        at = pl.ds(pl.multiple_of(tile * 96, 96), 96)
                        feature_rows[1, at, :] = close_rows[choice(), at, :]
                        return 0

                    lax.fori_loop(0, 4 * part // 96, take, 0)
                else:
                    for i in range(4):
                        text_copy(0, i).wait_recv()

            @pl.when(unit == 2)
            def _():
                for i in range(4):
                    near_on[i].wait_recv()
                    side_on[i].wait_recv()

            @pl.when(unit == 3)
            def _():
                near_rest.wait_recv()

        else:

            @pl.when(unit > 0)
            def _():
                for i in range(4):
                    text_copy(unit - 1, i).wait_recv()

        raw = lax.dot_general(
            feature_rows[unit], proj[...], FIRST, preferred_element_type=F32
        )
        text_raw[other] = raw

        def unit_text(tile, _):
            at = strip(tile)
            wide = text_raw[other, at, :]
            text_low[at, :] = (wide * inverse_norm(wide)).astype(BF16)
            text_dir[other, at, :] = jnp.zeros((STRIP, width), F32)
            return 0

        lax.fori_loop(0, share // STRIP, unit_text, 0)

        def step(tile, _):
            images = pl.ds(pl.multiple_of(tile * 2 * share, 2 * share), 2 * share)
            image = image_low[images, :]
            text = text_low[...]
            logits = scale * lax.dot_general(image, text, LAST, preferred_element_type=F32) + bias
            line = lax.broadcasted_iota(jnp.int32, logits.shape, 0)
            column = lax.broadcasted_iota(jnp.int32, logits.shape, 1)
            same = line - column == (slot - 2 * tile) * share - unit * 4 * rows
            value = scale / (1.0 + jnp.exp(jnp.where(same, logits, -logits)))
            coeffs = jnp.where(same, -value, value).astype(BF16)
            image_dir[images, :] += jnp.dot(coeffs, text, preferred_element_type=F32)
            text_dir[other] += lax.dot_general(coeffs, image, FIRST, preferred_element_type=F32)
            return 0

        lax.fori_loop(0, rows // (2 * share), step, 0)

        @pl.when(unit > 0)
        def _():
            def shorten(tile, _):
                grad_out[unit - 1, strip(tile), :] = text_dir[1, strip(tile), :].astype(BF16)
                return 0

            lax.fori_loop(0, share // STRIP, shorten, 0)
            if not stop:
                grad_copy(unit - 1, 0).start()
                grad_copy(unit - 1, 1).start()

        if stop:

            @pl.when(unit == 1)
            def _():
                for piece in range(2):
                    if merged:
                        for m in range(3):
                            close_grad(m, piece).start()
                    else:
                        grad_copy(0, piece).start()

            @pl.when(unit == 2)
            def _():
                near_back.start()
                side_back.start()

            @pl.when(unit == 3)
            def _():
                near_direct.start()

        return 0

    lax.fori_loop(0, 4, window, 0)

    outgoing_image(0, peer[3], False)
    reduce_far = copy(reduce_out.at[0], reduce_in.at[0], mates[1])
    reduce_far.start()
    outgoing_image(1, peer[1], False)
    reduce_core = copy(reduce_out.at[1], reduce_in.at[1], mates[1])
    reduce_core.start()
    reduce_far.wait_recv()
    outgoing_image(2, peer[2], True)
    reduce_cross = copy(reduce_out.at[2], reduce_in.at[2], mates[2])
    reduce_cross.start()

    if stop:
        side_back.wait_recv()
        side_passed.start()
        near_back.wait_recv()

        def add_on(tile, _):
            at = strip(tile)
            here = pl.ds(pl.multiple_of((1 - bit) * half + tile * STRIP, STRIP), STRIP)
            relay_out[at, :] = (text_dir[1, here, :] + relay_in[0, at, :].astype(F32)).astype(BF16)
            grad_in[1, pl.ds(pl.multiple_of(bit * half + tile * STRIP, STRIP), STRIP), :] = (
                jnp.zeros((STRIP, width), BF16)
            )
            return 0

        lax.fori_loop(0, half // STRIP, add_on, 0)
        near_sum.start()

    reduce_core.wait_recv()
    reduce_cross.wait_recv()

    def finish_image(tile, _):
        at = strip(tile)
        here = pl.ds(pl.multiple_of(slot * share + tile * STRIP, STRIP), STRIP)
        wide = image_ref[here, :].astype(F32)
        scaled = inverse_norm(wide)
        unit = wide * scaled
        total = image_dir[here, :] + reduce_in[1, at, :].astype(F32)
        total = total + reduce_in[2, at, :].astype(F32)
        total = total - unit * jnp.sum(unit * total, axis=1, keepdims=True)
        image_grad_ref[at, :] = total * scaled
        return 0

    lax.fori_loop(0, share // STRIP, finish_image, 0)

    def piece_in(turn):
        return turn * bit + (1 - turn) * (1 - bit) if stop else turn

    def finish_text(turn, _):
        piece = piece_in(turn)
        at = pl.ds(pl.multiple_of(piece * half, half), half)
        if stop:

            @pl.when(turn == 0)
            def _():
                for part_of in range(2):
                    if merged:
                        for m in range(3):
                            close_grad(m, part_of).wait_recv()
                    else:
                        grad_copy(0, part_of).wait_recv()
                near_direct.wait_recv()
                side_passed.wait_recv()

            @pl.when(turn == 1)
            def _():
                near_sum.wait_recv()

        else:
            for r in range(3):
                grad_copy(r, piece).wait_recv()

        def rows_done(tile, _):
            here = pl.ds(pl.multiple_of(piece * half + tile * STRIP, STRIP), STRIP)
            raw = text_raw[0, here, :]
            scaled = inverse_norm(raw)
            unit = raw * scaled
            first = close_in[choice(), here, :] if merged else grad_in[0, here, :]
            total = text_dir[0, here, :] + first.astype(F32)
            total = total + grad_in[1, here, :].astype(F32) + grad_in[2, here, :].astype(F32)
            total = total - unit * jnp.sum(unit * total, axis=1, keepdims=True)
            text_grad_ref[here, :] = total * scaled
            return 0

        lax.fori_loop(0, half // STRIP, rows_done, 0)
        values = lax.dot_general(
            proj[...], text_grad_ref[at, :].astype(BF16), LAST, preferred_element_type=F32
        )
        for i in (2, 3, 1):
            block_out[i - 1, :, lanes(turn)] = values[i * part : (i + 1) * part].astype(BF16)
            block_copy(i, turn).start()
        feature_grad_ref[:, piece_of(slot, piece)] = values[:part]
        return 0

    lax.fori_loop(0, 2, finish_text, 0)

    for turn in range(2):
        for i in (1, 2, 3):
            block_copy(i, turn).wait_recv()
            feature_grad_ref[:, piece_of(peer[i], piece_in(turn))] = block_in[
                i - 1, :, pl.ds(turn * half, half)
            ].astype(F32)

    for i in (1, 2, 3):
        features[i].wait_send()
        for piece in range(2):
            block_copy(i, piece).wait_send()
    if merged:
        for m in range(3):
            for i in range(4):
                close_text(m, i).wait_send()
            for piece in range(2):
                close_grad(m, piece).wait_send()
    for r in range(0 if merged else 1 if stop else 3):
        for i in range(4):
            text_copy(r, i).wait_send()
        for piece in range(2):
            grad_copy(r, piece).wait_send()
    if stop:
        for c in near_half + side_half + near_on + side_on:
            c.wait_send()
        for c in (near_rest, near_back, side_back, near_direct, near_sum, side_passed):
            c.wait_send()
    for c in (proj_core, proj_near, proj_wrap, pass_near, pass_wrap):
        c.wait_send()
    for c in (reduce_far, reduce_core, reduce_cross):
        c.wait_send()


def fused(number, near, scale, bias, masks, image, feature, projection):
    rows, width = image.shape
    part = feature.shape[0]
    share = rows // 4
    vmem = pl.BlockSpec(memory_space=pltpu.VMEM)
    smem = pl.BlockSpec(memory_space=pltpu.SMEM)
    any_space = pl.BlockSpec(memory_space=pl.ANY)
    semaphores = [36, 36, 12, 12, 6, 6, 6, 6, 3]
    return pl.pallas_call(
        functools.partial(kernel, near),
        out_shape=(
            jax.ShapeDtypeStruct((share, width), F32),
            jax.ShapeDtypeStruct((share, width), F32),
            jax.ShapeDtypeStruct((part, rows), F32),
        ),
        in_specs=[smem, smem, smem, any_space, any_space, any_space],
        out_specs=[vmem, vmem, vmem],
        scratch_shapes=[
            pltpu.VMEM((rows, width), BF16),
            pltpu.VMEM((rows, width), BF16),
            pltpu.VMEM((4 * part, width), BF16),
            pltpu.VMEM((4, 4 * part, share), BF16),
            pltpu.VMEM((2, share, width), F32),
            pltpu.VMEM((share, width), BF16),
            pltpu.VMEM((rows, width), F32),
            pltpu.VMEM((2, share, width), F32),
            pltpu.VMEM((3, share, width), BF16),
            pltpu.VMEM((3, share, width), BF16),
            pltpu.VMEM((3, share, width), BF16),
            pltpu.VMEM((3, share, width), BF16),
            pltpu.VMEM((3, part, share), BF16),
            pltpu.VMEM((3, part, share), BF16),
            pltpu.VMEM((4 * part, share // 2), BF16),
            pltpu.VMEM((2, share // 2, width), BF16),
            pltpu.VMEM((share // 2, width), BF16),
            pltpu.VMEM((3, 4 * part, share), BF16),
            pltpu.VMEM((3, share, width), BF16),
        ]
        + [pltpu.SemaphoreType.DMA((count,)) for count in semaphores],
        compiler_params=pltpu.CompilerParams(
            collective_id=number, has_side_effects=True, vmem_limit_bytes=56 * 1024 * 1024
        ),
    )(scale, bias, masks, image, feature, projection)


def per_device(image_embed, text_feature, projection, logit_scale, logit_bias, partner_masks):
    chosen = partner_masks[0] + partner_masks[1] + partner_masks[2] - FAR
    which = jnp.where(chosen == 24, 5, jnp.where(chosen > 16, 4, 3))
    which = jnp.where(chosen < 8, (chosen - 2) // 2, which)
    image_grad, text_grad, feature_grad = lax.switch(
        which,
        [functools.partial(fused, number, pair) for number, pair in enumerate(PAIRS)],
        logit_scale,
        logit_bias,
        partner_masks,
        image_embed,
        text_feature.T,
        projection,
    )
    return (image_grad, text_grad, feature_grad.T)


def solution(mesh):
    return jax.shard_map(
        per_device,
        mesh=mesh,
        in_specs=(P("dp", None), P("dp", "tensor"), P("tensor", None), P(), P(), P()),
        out_specs=(P(("dp", "tensor"), None), P(("dp", "tensor"), None), P("dp", "tensor")),
        check_vma=False,
    )
```
